512 devices in a mesh: grid: 64 (over z_lo, y, core), orb: 8 (over z_hi, x).
Axes of the slice: x: 4, y: 4, z: 16 (z_hi: 2, z_lo: 8; z = z_hi * 8 + z_lo), core: 2. Of those that a mesh axis runs over, the one named last changes fastest.
Arguments:
- occupied: bfloat16 [80, 6400, 1024], P(None, 'grid', 'orb'), may hold values from -6 to 6
- virtual: bfloat16 [80, 6400, 1024], P(None, 'grid', 'orb'), may hold values from -6 to 6
- points: int32 [128], replicated, may hold values from 0 to 511999, as said below
- panels: int32 [2, 64], replicated, may hold values from 0 to 127, as said below
Outputs:
- projection: float32 [64, 64], P('orb')
The draws below stay inside these ranges and needn't reach their ends.
Inputs may be any that keep to these rules, and one draw needn't show every extreme that they name: `points`: the 128 cells are distinct. Every index of points appears exactly once in panels, so the two panels are disjoint.
All inputs are finite; a program needn't handle non-finite values.
Results may differ from the reference program's by a relative error of at most 0.0003.
Values may be sent and summed in bfloat16 or wider, within the bound.
No kernel may reach another device: no remote copies, remote signals or barrier semaphores. Data moves between devices by JAX's collectives and lax.ppermute only.
A program may use at most 64 MiB of HBM per device.

```python
import math
import jax
import jax.numpy as jnp
from jax import lax

NA = 80
NB = 80
NC = 80
NOCC = 1024
NVIR = 1024
PANEL = 64
NBC = 6400
NPTS = 128


def draw_points(key, part):
    key = jax.random.fold_in(key, 17)
    cell_count = NA * NB * NC
    first_key, second_key = jax.random.split(key)
    interior = jax.random.permutation(first_key, cell_count - 2)[:NPTS - 2] + 1
    extremes = jnp.array([0, cell_count - 1], dtype=jnp.int32)
    chosen = jnp.concatenate([extremes, interior.astype(jnp.int32)])
    return chosen[jax.random.permutation(second_key, NPTS)].astype(jnp.int32)


def draw_panels(key, part):
    key = jax.random.fold_in(key, 29)
    return jax.random.permutation(key, NPTS).astype(jnp.int32).reshape(2, PANEL)


def shard_levels(key, shape, shards, low, top_value):
    gain, own = 1.0, jax.random.fold_in(key, 6)
    for position, parts in shards:
        draws = jnp.exp(jax.random.uniform(jax.random.fold_in(own, position), (parts,), jnp.float32, low / len(shards), top_value / len(shards)))
        gain = gain * jnp.repeat(draws, shape[position] // parts).reshape([-1 if axis == position else 1 for axis in range(len(shape))])
    return gain


def bell_draw(own_key, dims, scale, most, shards=(), held_as=jnp.bfloat16):
    drawn = jax.random.normal(own_key, dims, jnp.float32) * scale
    if len(shards) > 0:
        drawn = shard_levels(own_key, dims, shards, -0.22, 0.18) * drawn
    return jnp.clip(drawn, min=-most, max=most).astype(held_as)


def setup_inputs(seed: int = 0) -> dict:
    streams_of = jax.random.split(jax.random.key(seed), 5)
    return {
        "occupied": bell_draw(streams_of[0], (NA, NBC, NOCC), 1.0, 6.0, ((1, 64), (2, 8))),
        "virtual": bell_draw(streams_of[1], (NA, NBC, NVIR), 1.0, 6.0, ((1, 64), (2, 8))),
        "points": draw_points(jax.random.fold_in(streams_of[4], 71), 0),
        "panels": draw_panels(jax.random.fold_in(streams_of[4], 71), 0),
    }


FOUR_PI = 4.0 * math.pi
TWO_PI = 2.0 * math.pi

def signed_square(length):
    steps = jnp.arange(length, dtype=jnp.int32)
    shifted = jnp.where(steps > length // 2, steps - length, steps).astype(jnp.float32)
    wave = TWO_PI / length * shifted
    return wave * wave

def kernel_grid():
    squared = signed_square(NA)[:, None, None] + signed_square(NB)[None, :, None] + signed_square(NC)[None, None, :]
    positive = jnp.where(squared > 0, squared, 1.0)
    return jnp.where(squared > 0, FOUR_PI / positive, 0.0)

def gram_solve(factor, values):
    lowered = lax.linalg.triangular_solve(factor, values, left_side=True, lower=True)
    return lax.linalg.triangular_solve(factor, lowered, left_side=True, lower=True, transpose_a=True)

def reference(occupied, virtual, points, panels):
    cell_count = NA * NB * NC
    flat_occ = occupied.reshape(cell_count, NOCC)
    flat_vir = virtual.reshape(cell_count, NVIR)
    chosen = points[panels.reshape(-1)]
    occ_pts = flat_occ[chosen]
    vir_pts = flat_vir[chosen]

    def hadamard_gram(start):
        occ_part = occ_pts[start:start + PANEL]
        vir_part = vir_pts[start:start + PANEL]
        return jnp.dot(occ_part.astype(jnp.float32), occ_part.T.astype(jnp.float32), preferred_element_type=jnp.float32) * jnp.dot(vir_part.astype(jnp.float32), vir_part.T.astype(jnp.float32), preferred_element_type=jnp.float32)
    chol_fit = jnp.linalg.cholesky(hadamard_gram(0))
    chol_bra = jnp.linalg.cholesky(hadamard_gram(PANEL))

    def fit_plane(plane_index):
        occ_rows = lax.dynamic_index_in_dim(occupied, plane_index, 0, keepdims=False)
        vir_rows = lax.dynamic_index_in_dim(virtual, plane_index, 0, keepdims=False)
        pairs = jnp.dot(occ_rows.astype(jnp.float32), occ_pts.T.astype(jnp.float32), preferred_element_type=jnp.float32) * jnp.dot(vir_rows.astype(jnp.float32), vir_pts.T.astype(jnp.float32), preferred_element_type=jnp.float32)
        return (gram_solve(chol_fit, pairs[:, :PANEL].T), gram_solve(chol_bra, pairs[:, PANEL:].T))
    fit_cols, bra_cols = lax.map(fit_plane, jnp.arange(NA, dtype=jnp.int32))
    fields = jnp.transpose(fit_cols, (1, 0, 2)).reshape(PANEL, NA, NB, NC)
    bra_all = jnp.transpose(bra_cols, (1, 0, 2)).reshape(PANEL, cell_count)
    kernel = kernel_grid()

    def poisson(scalar_field):
        return jnp.real(jnp.fft.ifftn(jnp.fft.fftn(scalar_field) * kernel)).astype(jnp.float32)
    potential = lax.map(poisson, fields).reshape(PANEL, cell_count)
    return 32.0 * jnp.dot(bra_all.astype(jnp.float32), potential.T.astype(jnp.float32), precision=lax.Precision.HIGHEST, preferred_element_type=jnp.float32)
```

```python
import math

import jax
import jax.numpy as jnp
import numpy as np
from jax import lax
from jax.sharding import Mesh, PartitionSpec as P

N = 80
PANEL = 64
GRID = ("zl", "yh", "yl", "c")
ORB = ("zh", "x")
PLANE = ("yl", "c", "x")
RING = ("yh", "zl", "zh")
BF16 = jnp.bfloat16
F32 = jnp.float32
FOUR_PI = 4.0 * math.pi
TWO_PI = 2.0 * math.pi


def real_basis():
    steps = np.arange(N)
    freqs = np.concatenate([np.arange(N // 2 + 1), np.arange(1, N // 2)])
    angle = TWO_PI / N * (freqs[:, None] * steps[None, :] % N)
    table = np.where(np.arange(N)[:, None] <= N // 2, np.cos(angle), np.sin(angle)) * math.sqrt(2.0 / N)
    table[0] /= math.sqrt(2.0)
    table[N // 2] /= math.sqrt(2.0)
    return table.astype(np.float32)


def freq_square(index):
    freq = jnp.where(index > N // 2, index - N // 2, index).astype(F32)
    wave = TWO_PI / N * freq
    return wave * wave


def mix(form, left, right):
    return jnp.einsum(form, left, right, precision=lax.Precision.HIGHEST, preferred_element_type=F32)


def swap(values, axes):
    return lax.all_to_all(values, axes, 0, 0, tiled=True)


def shards(occupied, virtual, points, panels):
    x_rank = lax.axis_index("x")
    zh_rank = lax.axis_index("zh")
    grid_rank = lax.axis_index(GRID)
    columns = occupied.shape[1]
    width = occupied.shape[2]
    per_x = columns // 4

    chosen = points[panels.reshape(-1)]
    plane_of = chosen // (N * N)
    within = chosen % (N * N) - grid_rank * columns
    inside = (within >= 0) & (within < columns)
    column_of = jnp.where(inside, within, 0)
    here = jnp.concatenate([occupied[plane_of, column_of], virtual[plane_of, column_of]], axis=1)
    here = jnp.where(inside[:, None], here, jnp.zeros((), BF16))
    two_rows = jnp.sum(swap(here.reshape(64, 2, 2 * width), GRID).astype(F32), axis=0).astype(BF16)
    gathered = swap(jnp.broadcast_to(two_rows[None], (256, 2, 2 * width)), GRID + ("x",))
    pts = gathered.reshape(64, 4, 2, 2 * width).transpose(1, 0, 2, 3).reshape(4, 2 * PANEL, 2 * width)

    def spread(array):
        parts = array.reshape(N, 4, per_x, width).transpose(1, 2, 0, 3).reshape(4, per_x * N, width)
        blocks = [lax.dynamic_index_in_dim(parts, x_rank, 0, keepdims=False)]
        for shift in (1, 3, 2):
            out = lax.dynamic_index_in_dim(parts, (x_rank + shift) % 4, 0, keepdims=False)
            blocks.append(lax.ppermute(out, "x", [(i, (i + shift) % 4) for i in range(4)]))
        return blocks

    occ_blocks = spread(occupied)
    vir_blocks = spread(virtual)
    pts_blocks = [lax.dynamic_index_in_dim(pts, (x_rank - shift) % 4, 0, keepdims=False) for shift in (0, 1, 3, 2)]

    def side_sums(start):
        rows = [lax.dynamic_slice_in_dim(block, start, PANEL, 0) for block in pts_blocks]

        def total(blocks, low):
            cells = jnp.concatenate(
                [jnp.concatenate([b, r[:, low : low + width]], axis=0) for b, r in zip(blocks, rows)], axis=1
            )
            weights = jnp.concatenate([r[:, low : low + width] for r in rows], axis=1)
            return jnp.dot(cells, weights.T, preferred_element_type=F32)

        return jnp.concatenate([total(occ_blocks, 0), total(vir_blocks, width)], axis=1)

    theirs = side_sums((1 - zh_rank) * PANEL)
    other = lax.ppermute(theirs, "zh", [(0, 1), (1, 0)])
    mine = side_sums(zh_rank * PANEL) + other
    pairs = mine[:, :PANEL] * mine[:, PANEL:]
    cell_count = per_x * N
    gram = pairs[cell_count:]
    factor = jnp.linalg.cholesky(gram)
    lowered = lax.linalg.triangular_solve(factor, jnp.eye(PANEL, dtype=F32), left_side=True, lower=True)
    inverse = mix("km,kn->mn", lowered, lowered)

    basis = real_basis()
    fields = pairs[:cell_count].reshape(per_x, N, PANEL)
    fields = mix("ka,caf->kcf", basis, fields).reshape(16, 5, per_x, PANEL)
    fields = swap(fields, PLANE)
    fields = fields.transpose(1, 0, 2, 3).reshape(5, 5, N, PANEL)
    fields = mix("qc,kbcf->kqbf", basis, fields)
    fields = mix("kqbf,fg->kqbg", fields, inverse).reshape(5 * N, 5, PANEL)
    fields = jnp.pad(fields, ((0, 16), (0, 0), (0, 0))).reshape(32, 13, 5, PANEL)
    fields = swap(fields, RING).reshape(2, 8, 2, 13, 5, PANEL)
    basis_b = basis.reshape(N, 8, 2, 5).transpose(0, 2, 1, 3)
    fields = mix("kyzb,yzhqbf->hqkf", basis_b, fields)

    slot = lax.axis_index(RING) * 13 + jnp.arange(13, dtype=jnp.int32)
    ka = lax.axis_index(PLANE) * 5 + slot // N
    squared = (freq_square(ka) + freq_square(slot % N))[:, None] + freq_square(jnp.arange(N, dtype=jnp.int32))[None, :]
    live = (squared > 0) & (slot < 5 * N)[:, None]
    kernel = jnp.where(live, 32.0 * FOUR_PI / jnp.where(squared > 0, squared, 1.0), 0.0)
    part = mix("qkm,qkn->mn", fields[1], fields[0] * kernel[:, :, None])
    part = jnp.sum(swap(part.reshape(8, 8, PANEL), ORB), axis=0)
    part = swap(jnp.broadcast_to(part[None], (64, 8, PANEL)), GRID)
    return jnp.sum(part, axis=0)


def solution(mesh):
    devices = mesh.devices.reshape(8, 2, 2, 2, 2, 4)
    inner = Mesh(devices, ("zl", "yh", "yl", "c", "zh", "x"))
    in_specs = (P(None, GRID, ORB), P(None, GRID, ORB), P(), P())
    return jax.shard_map(shards, mesh=inner, in_specs=in_specs, out_specs=P(ORB, None), check_vma=False)
```

```python
import math

import jax
import jax.numpy as jnp
import numpy as np
from jax import lax
from jax.sharding import Mesh, PartitionSpec as P

N = 80
PANEL = 64
GRID = ("zl", "yh", "yl", "c")
ORB = ("zh", "x")
ROWS = ("yh", "yl", "c")
PLANE = ("yl", "c", "x")
RING = ("yh", "zl", "zh")
BF16 = jnp.bfloat16
F32 = jnp.float32
F16 = jnp.float16
SPAN = 5.21
FOUR_PI = 4.0 * math.pi
TWO_PI = 2.0 * math.pi


def real_basis():
    steps = np.arange(N)
    freqs = np.concatenate([np.arange(N // 2 + 1), np.arange(1, N // 2)])
    angle = TWO_PI / N * (freqs[:, None] * steps[None, :] % N)
    table = np.where(np.arange(N)[:, None] <= N // 2, np.cos(angle), np.sin(angle)) * math.sqrt(2.0 / N)
    table[0] /= math.sqrt(2.0)
    table[N // 2] /= math.sqrt(2.0)
    return table.astype(np.float32)


def freq_square(index):
    freq = jnp.where(index > N // 2, index - N // 2, index).astype(F32)
    wave = TWO_PI / N * freq
    return wave * wave


def mix(form, left, right):
    return jnp.einsum(form, left, right, precision=lax.Precision.HIGHEST, preferred_element_type=F32)


def swap(values, axes):
    return lax.all_to_all(values, axes, 0, 0, tiled=True)


def encode(values):
    square = jnp.mean(values * values, axis=0, keepdims=True)
    power = jnp.ceil(0.5 * jnp.log2(jnp.maximum(square, 1e-37))) - 1.0
    size = jnp.abs(values) * jnp.exp2(-power)
    level = jnp.log(size + jnp.sqrt(size * size + 1.0)) * (29.98 / SPAN)
    whole = jnp.floor(level)
    code = jnp.exp2(whole - 14.0) * (1.0 + (level - whole))
    return jnp.where(values < 0, -code, code).astype(F16), power.astype(F16)


def decode(code, power):
    code = code.astype(F32)
    size = jnp.abs(code)
    whole = jnp.floor(jnp.log2(size) + 2e-4)
    level = whole + (size * jnp.exp2(-whole) - 1.0) + 14.0
    spread = jnp.exp(level * (SPAN / 29.98))
    value = 0.5 * (spread - 1.0 / spread) * jnp.exp2(power.astype(F32))
    return jnp.where(code < 0, -value, value)


def shards(occupied, virtual, points, panels):
    x_rank = lax.axis_index("x")
    zh_rank = lax.axis_index("zh")
    grid_rank = lax.axis_index(GRID)
    columns = occupied.shape[1]
    width = occupied.shape[2]
    per_x = columns // 4

    chosen = points[panels.reshape(-1)]
    plane_of = chosen // (N * N)
    within = chosen % (N * N) - grid_rank * columns
    inside = (within >= 0) & (within < columns)
    column_of = jnp.where(inside, within, 0)
    here = jnp.concatenate([occupied[plane_of, column_of], virtual[plane_of, column_of]], axis=1)
    here = jnp.where(inside[:, None], here, jnp.zeros((), BF16))

    parts = jnp.concatenate([occupied, virtual], axis=2).reshape(N, 4, per_x, 2 * width)
    parts = parts.transpose(1, 2, 0, 3).reshape(4, per_x * N, 2 * width)

    def take(shift):
        return lax.dynamic_index_in_dim(parts, (x_rank + shift) % 4, 0, keepdims=False)

    def spread(block, shift):
        return lax.ppermute(block, "x", [(i, (i + shift) % 4) for i in range(4)])

    far = take(2)
    half = far.shape[0] // 2
    blocks = {0: take(0), 1: spread(take(1), 1), 3: spread(take(3), 3)}
    far_low = spread(far[:half], 2)

    def add(values):
        return jnp.sum(values.astype(F32), axis=0).astype(BF16)

    rows = add(swap(here.reshape(8, 16, 2 * width), ROWS))
    rows = add(swap(jnp.broadcast_to(rows[None], (8, 16, 2 * width)), "zl"))
    rows, blocks[1], blocks[3], far_low = lax.optimization_barrier((rows, blocks[1], blocks[3], far_low))
    blocks[2] = jnp.concatenate([far_low, spread(far[half:], 2)], axis=0)
    gathered = swap(jnp.broadcast_to(rows[None], (32, 16, 2 * width)), ROWS + ("x",))
    pts = gathered.reshape(8, 4, 16, 2 * width).transpose(1, 0, 2, 3).reshape(4, 2 * PANEL, 2 * width)
    shifts = (0, 1, 3, 2)
    pts_blocks = [lax.dynamic_index_in_dim(pts, (x_rank - shift) % 4, 0, keepdims=False) for shift in shifts]

    def side_weights(start):
        heads, tables = [], []
        gap = jnp.zeros((PANEL, width), BF16)
        for block in pts_blocks:
            head = lax.dynamic_slice_in_dim(block, start, PANEL, 0)
            upper = jnp.concatenate([head[:, :width], gap], axis=1)
            lower = jnp.concatenate([gap, head[:, width:]], axis=1)
            heads.append(head)
            tables.append(jnp.concatenate([upper, lower], axis=0))
        return heads, tables

    def side_sums(cells, tables):
        return sum(jnp.dot(c, t.T, preferred_element_type=F32) for c, t in zip(cells, tables))

    def cross(values):
        return lax.ppermute(values, "zh", [(0, 1), (1, 0)])

    their_heads, their_tables = side_weights((1 - zh_rank) * PANEL)
    my_heads, my_tables = side_weights(zh_rank * PANEL)
    cells = [blocks[shift] for shift in shifts]
    gram = side_sums(my_heads, my_tables) + cross(side_sums(their_heads, their_tables))
    factor = jnp.linalg.cholesky(gram[:, :PANEL] * gram[:, PANEL:])
    lowered = lax.linalg.triangular_solve(factor, jnp.eye(PANEL, dtype=F32), left_side=True, lower=True)
    inverse = mix("km,kn->mn", lowered, lowered)

    cell_count = per_x * N
    code, power = encode(side_sums(cells, their_tables))
    sent = jnp.concatenate([code, jnp.broadcast_to(power, (16, 2 * PANEL))], axis=0)
    got = cross(sent)
    mine = side_sums(cells, my_tables)
    got, inverse, mine = lax.optimization_barrier((got, inverse, mine))
    mine = mine + decode(got[:cell_count], got[cell_count : cell_count + 1])
    pairs = mine[:, :PANEL] * mine[:, PANEL:]

    basis = real_basis()
    fields = pairs.reshape(per_x, N, PANEL)
    fields = mix("ka,caf->kcf", basis, fields).reshape(16, 5, per_x, PANEL)
    fields = swap(fields, PLANE)
    fields = fields.transpose(1, 0, 2, 3).reshape(5, 5, N, PANEL)
    fields = mix("qc,kbcf->kqbf", basis, fields)
    fields = mix("kqbf,fg->kqbg", fields, inverse).reshape(25 * N, PANEL)
    code, power = encode(fields)
    code = jnp.concatenate([code, jnp.ones((80, PANEL), F16)], axis=0).reshape(32, 65, PANEL)
    power = jnp.broadcast_to(power[None], (32, 1, PANEL))
    sent = jnp.concatenate([code[:, :33], jnp.concatenate([code[:, 33:], power], axis=1)], axis=2)
    got = swap(sent, RING)
    power = got[:, 32:, PANEL:]
    fields = jnp.concatenate([decode(got[:, :, :PANEL], power), decode(got[:, :32, PANEL:], power)], axis=1)
    fields = fields.reshape(2, 8, 2, 13, 5, PANEL)
    basis_b = basis.reshape(N, 8, 2, 5).transpose(0, 2, 1, 3)
    fields = mix("kyzb,yzhqbf->hqkf", basis_b, fields)

    slot = lax.axis_index(RING) * 13 + jnp.arange(13, dtype=jnp.int32)
    ka = lax.axis_index(PLANE) * 5 + slot // N
    squared = (freq_square(ka) + freq_square(slot % N))[:, None] + freq_square(jnp.arange(N, dtype=jnp.int32))[None, :]
    live = (squared > 0) & (slot < 5 * N)[:, None]
    kernel = jnp.where(live, 32.0 * FOUR_PI / jnp.where(squared > 0, squared, 1.0), 0.0)
    part = mix("qkm,qkn->mn", fields[1], fields[0] * kernel[:, :, None])
    part = part.reshape(2, 4, 8, PANEL).transpose(1, 0, 2, 3)
    part = jnp.broadcast_to(part[None], (8, 4, 2, 8, PANEL)).reshape(32, 16, PANEL)
    part = jnp.sum(swap(part, ROWS + ("x",)), axis=0)
    part = jnp.broadcast_to(part.reshape(1, 2, 8, PANEL), (8, 2, 8, PANEL)).reshape(16, 8, PANEL)
    return jnp.sum(swap(part, ("zl", "zh")), axis=0)


def solution(mesh):
    devices = mesh.devices.reshape(8, 2, 2, 2, 2, 4)
    inner = Mesh(devices, ("zl", "yh", "yl", "c", "zh", "x"))
    in_specs = (P(None, GRID, ORB), P(None, GRID, ORB), P(), P())
    return jax.shard_map(shards, mesh=inner, in_specs=in_specs, out_specs=P(ORB, None), check_vma=False)
```

```python
import math

import jax
import jax.numpy as jnp
import ml_dtypes
import numpy as np
from jax import lax
from jax.experimental import pallas as pl
from jax.experimental.pallas import tpu as pltpu
from jax.sharding import Mesh, PartitionSpec as P

N = 80
PANEL = 64
GRID = ("zl", "yh", "yl", "c")
ORB = ("zh", "x")
ROWS = ("yh", "yl", "c")
PLANE = ("yl", "c", "x")
RING = ("yh", "zl", "zh")
BF16 = jnp.bfloat16
F32 = jnp.float32
LEVELS = 252.9
SPAN = 5.21
SHIFTS = (0, 1, 3, 2)
TILE = 400
CELLS = 2000
FOUR_PI = 4.0 * math.pi
TWO_PI = 2.0 * math.pi


def real_basis():
    steps = np.arange(N)
    freqs = np.concatenate([np.arange(N // 2 + 1), np.arange(1, N // 2)])
    angle = TWO_PI / N * (freqs[:, None] * steps[None, :] % N)
    table = np.where(np.arange(N)[:, None] <= N // 2, np.cos(angle), np.sin(angle)) * math.sqrt(2.0 / N)
    table[0] /= math.sqrt(2.0)
    table[N // 2] /= math.sqrt(2.0)
    return table.astype(np.float32)


def freq_square(index):
    freq = jnp.where(index > N // 2, index - N // 2, index).astype(F32)
    wave = TWO_PI / N * freq
    return wave * wave


def mix(form, left, right):
    return jnp.einsum(form, left, right, precision=lax.Precision.HIGHEST, preferred_element_type=F32)


def swap(values, axes):
    return lax.all_to_all(values, axes, 0, 0, tiled=True)


def lane_power(square_sum, count):
    return jnp.ceil(0.5 * jnp.log2(jnp.maximum(square_sum * (1.0 / count), 1e-37))) - 1.0


def encode(values, power):
    size = jnp.abs(values) * jnp.exp2(-power)
    level = jnp.log(size + jnp.sqrt(size * size + 1.0)) * (LEVELS / SPAN)
    whole = jnp.floor(level)
    code = jnp.exp2(whole - 126.0) * (1.0 + (level - whole))
    return jnp.where(values < 0, -code, code)


def decode(code, power):
    size = jnp.abs(code)
    whole = jnp.floor(jnp.log2(size) + 1e-3)
    level = whole + (size * jnp.exp2(-whole) - 1.0) + 126.0
    spread = jnp.exp(level * (SPAN / LEVELS))
    value = 0.5 * (spread - 1.0 / spread) * jnp.exp2(power)
    return jnp.where(code < 0, -value, value)


def whole_call(kernel, out_shape, scratch, scalars, *arrays):
    vmem = pl.BlockSpec(memory_space=pltpu.VMEM)
    shapes = [a.shape for a in arrays]
    moved = sum(math.prod(shape) * 4 for shape in shapes)
    return pl.pallas_call(
        kernel,
        out_shape=out_shape,
        in_specs=[pl.BlockSpec(memory_space=pltpu.SMEM)] * len(scalars) + [vmem] * len(arrays),
        out_specs=jax.tree.map(lambda _: vmem, out_shape),
        scratch_shapes=scratch,
        compiler_params=pltpu.CompilerParams(vmem_limit_bytes=40 * 2**20),
        cost_estimate=pl.CostEstimate(flops=2 * 10**9, bytes_accessed=moved, transcendentals=0),
    )(*scalars, *arrays)


def head_rows(points_ref, shift, x_rank, panel):
    block = lax.rem(x_rank - shift + 4, 4)
    return jnp.concatenate([points_ref[(panel * 4 + i) * 4 + block] for i in range(4)], axis=0)


def side_table(head):
    half = head.shape[1] // 2
    gap = jnp.zeros((head.shape[0], half), head.dtype)
    upper = jnp.concatenate([head[:, :half], gap], axis=1)
    lower = jnp.concatenate([gap, head[:, half:]], axis=1)
    return jnp.concatenate([upper, lower], axis=0)


def dot_rows(left, right, precision=None):
    return lax.dot_general(left, right, (((1,), (1,)), ((), ())), precision=precision, preferred_element_type=F32)


def split(values):
    high = values.astype(BF16)
    return high, (values - high.astype(F32)).astype(BF16)


def dot_two(table_ref, values):
    high, low = split(values)
    count = table_ref.shape[0] // 2
    top, rest = table_ref[pl.ds(0, count), :], table_ref[pl.ds(count, count), :]
    return dot(top, high) + (dot(top, low) + dot(rest, high))


def dot(left, right):
    return lax.dot_general(left, right, (((1,), (0,)), ((), ())), preferred_element_type=F32)


def two_parts(table):
    high = table.astype(ml_dtypes.bfloat16)
    low = (table - high.astype(np.float32)).astype(ml_dtypes.bfloat16)
    return jnp.asarray(np.concatenate([high, low], axis=0))


def cell_tiles(blocks):
    own, left, right, far_low, far_high = blocks
    for tile in range(5):
        rows = pl.ds(tile * TILE, TILE)
        far = far_low[rows, :] if tile < 3 else far_high[pl.ds((tile - 3) * TILE, TILE), :]
        yield rows, (own[rows, :], left[rows, :], right[rows, :], far)


def sums_kernel(rank_ref, points_ref, own, left, right, far_low, far_high, up_ref, down_ref, sum_ref):
    half = rank_ref[1]
    tables = []
    for shift in SHIFTS:
        heads = [head_rows(points_ref, shift, rank_ref[0], panel) for panel in (half, 1 - half)]
        tables.append(jnp.concatenate([side_table(head) for head in heads], axis=0))
    square = jnp.zeros((1, 4 * PANEL), F32)
    for rows, parts in cell_tiles((own, left, right, far_low, far_high)):
        total = sum(dot_rows(part, table) for part, table in zip(parts, tables))
        sum_ref[rows, :] = total
        square = square + jnp.sum(total * total, axis=0, keepdims=True)
    power = lane_power(square, CELLS)
    for out_ref, low in ((up_ref, 0), (down_ref, 2 * PANEL)):
        lanes = pl.ds(low, 2 * PANEL)
        own_power = power[:, low : low + 2 * PANEL]
        for tile in range(5):
            rows = pl.ds(tile * TILE, TILE)
            out_ref[rows, :] = encode(sum_ref[rows, lanes], own_power).astype(BF16)
        out_ref[pl.ds(CELLS, 16), :] = jnp.broadcast_to(own_power, (16, 2 * PANEL)).astype(BF16)


def gram_kernel(rank_ref, points_ref, gram_ref, other_ref):
    for out_ref, panel in ((gram_ref, rank_ref[2]), (other_ref, 1 - rank_ref[2])):
        heads = [head_rows(points_ref, shift, rank_ref[0], panel) for shift in SHIFTS]
        out_ref[...] = sum(dot_rows(head, side_table(head)) for head in heads)


def first_kernel(below_ref, above_ref, basis_ref, out_ref):
    powers = [ref[pl.ds(CELLS, 16), :].astype(F32)[:1] for ref in (below_ref, above_ref)]
    left_lanes = lax.broadcasted_iota(jnp.int32, (N, 2 * PANEL), 1) < PANEL
    out_ref[...] = jnp.zeros_like(out_ref)

    def product(column):
        rows = pl.ds(column * N, N)
        sums = decode(below_ref[rows, :].astype(F32), powers[0]) + decode(above_ref[rows, :].astype(F32), powers[1])
        return sums * pltpu.roll(sums, PANEL, 1)

    pairs = []
    for pair in range(13):
        right = product(pair + 13) if pair < 12 else 0.0
        pairs.append(jnp.where(left_lanes, product(pair), right))
    moved = dot_two(basis_ref, jnp.concatenate(pairs, axis=1))
    for pair in range(13):
        for k in range(5):
            rows = moved[k * 16 : k * 16 + 16, pair * 2 * PANEL : (pair + 1) * 2 * PANEL]
            out_ref[pl.ds(k * 16 + pair, 16, stride=80), :] = rows


def inverse_kernel(mine_ref, other_ref, out_ref):
    sums = mine_ref[...] + other_ref[...]
    matrix = sums * pltpu.roll(sums, PANEL, 1)
    lane = lax.broadcasted_iota(jnp.int32, (PANEL, 2 * PANEL), 1)
    line = lax.broadcasted_iota(jnp.int32, (PANEL, 2 * PANEL), 0)
    for step in range(PANEL):
        scale = 1.0 / matrix[step : step + 1, step : step + 1]
        row = jnp.where(lane[:1] == step, 1.0, matrix[step : step + 1]) * scale
        column = matrix[:, step : step + 1]
        rest = jnp.where(lane == step, 0.0, matrix) - column * row
        matrix = jnp.where(line == step, row, rest)
    out_ref[pl.ds(0, PANEL), :] = jnp.where(lane < PANEL, matrix, 0.0)
    out_ref[pl.ds(PANEL, PANEL), :] = jnp.where(lane < PANEL, 0.0, pltpu.roll(matrix, PANEL, 1))


def second_kernel(in_ref, table_ref, inverse_ref, out_ref, line_ref, code_ref):
    left_lanes = lax.broadcasted_iota(jnp.int32, (200, 2 * PANEL), 1) < PANEL
    data = [in_ref[:, pl.ds(k * 16, 16), :].reshape(256, 2 * PANEL) for k in range(5)]
    moved = dot_two(table_ref, jnp.concatenate(data, axis=1))
    inverse = split(inverse_ref[...])
    square = jnp.zeros((1, 2 * PANEL), F32)
    for k in range(5):
        part = moved[:, k * 2 * PANEL : (k + 1) * 2 * PANEL]
        low = part[:200] + pltpu.roll(part[200:400], PANEL, 1)
        high = pltpu.roll(part[400:600], PANEL, 1) + part[600:]
        top, rest = split(jnp.where(left_lanes, low, high))
        mixed = dot(top, inverse[0]) + (dot(top, inverse[1]) + dot(rest, inverse[0]))
        line_ref[pl.ds(k * 200, 200), :] = mixed
        square = square + jnp.sum(mixed * mixed, axis=0, keepdims=True)
    power = lane_power(square, 1000)
    line_ref[pl.ds(1000, 120), :] = jnp.zeros((120, 2 * PANEL), F32)
    for tile in range(4):
        rows = pl.ds(tile * 280, 280)
        line_ref[rows, :] = encode(line_ref[rows, :], power)
    for to in range(32):
        code_ref[pl.ds(40 * to, 35), :] = line_ref[pl.ds(35 * to, 35), :]
        code_ref[pl.ds(40 * to + 35, 5), :] = jnp.broadcast_to(power, (5, 2 * PANEL))
    for tile in range(4):
        rows = pl.ds(tile * 320, 320)
        out_ref[rows, :] = code_ref[rows, :].astype(BF16)


def third_kernel(got_ref, table_ref, kernel_ref, out_ref):
    keep = lax.broadcasted_iota(jnp.int32, (40, 2 * PANEL), 0) < 35

    def side(panel):
        parts = []
        for source in range(16):
            block = got_ref[2 * source + (panel + (source % 8 < 4)) % 2].astype(F32)
            parts.append(jnp.where(keep, decode(jnp.where(keep, block, 1.0), block[35:36]), 0.0))
        return jnp.concatenate(parts, axis=0)

    moved = dot_two(table_ref, jnp.concatenate([side(0), side(1)], axis=1))
    fit_top, fit_rest = split(moved[:, : 2 * PANEL] * kernel_ref[...])
    bra_top, bra_rest = split(moved[:, 2 * PANEL :])

    def meet(left, right):
        return lax.dot_general(left, right, (((0,), (0,)), ((), ())), preferred_element_type=F32)

    total = meet(bra_top, fit_top) + (meet(bra_top, fit_rest) + meet(bra_rest, fit_top))
    out_ref[...] = total[:PANEL, :PANEL] + total[PANEL:, PANEL:]


def second_table():
    basis = real_basis().astype(np.float64)
    full = np.zeros((N, 5, 5 * N))
    for row in range(5):
        full[:, row, row * N : (row + 1) * N] = basis
    full = full.reshape(2, 200, 16, 25)
    table = np.zeros((2, 2, 200, 16, 16))
    table[:, 0, :, :, :13] = full[..., :13]
    table[:, 1, :, :, :12] = full[..., 13:]
    return table.reshape(800, 256).astype(np.float32)


def third_table():
    basis = np.roll(real_basis().reshape(N, 8, 2, 5).transpose(0, 2, 1, 3), 4, axis=2)
    table = np.zeros((7, N, 2, 8, 40), np.float32)
    for pair in range(7):
        table[pair, ..., pair * 5 : pair * 5 + 5] = basis
    return table.reshape(7 * N, 640)


def shards(occupied, virtual, points, panels):
    x_rank = lax.axis_index("x")
    zh_rank = lax.axis_index("zh")
    grid_rank = lax.axis_index(GRID)
    columns = occupied.shape[1]
    width = occupied.shape[2]
    per_x = columns // 4

    parts = jnp.concatenate([occupied, virtual], axis=2).reshape(N, 4, per_x, 2 * width)
    parts = parts.transpose(1, 2, 0, 3).reshape(4, per_x * N, 2 * width)

    wanted = panels.reshape(-1, 1) == jnp.arange(2 * PANEL, dtype=jnp.int32)
    chosen = jnp.sum(jnp.where(wanted, points, 0), axis=1)
    within = chosen % (N * N) - grid_rank * columns
    inside = (within >= 0) & (within < columns)
    plane_of = chosen // (N * N)
    column_of = jnp.where(inside, within, 0)
    here = jnp.concatenate([occupied[plane_of, column_of], virtual[plane_of, column_of]], axis=1)
    here = jnp.where(inside[:, None], here, jnp.zeros((), BF16))

    def take(shift):
        return lax.dynamic_index_in_dim(parts, (x_rank + shift) % 4, 0, keepdims=False)

    def spread(block, shift):
        return lax.ppermute(block, "x", [(i, (i + shift) % 4) for i in range(4)])

    far = take(2)
    split = 3 * TILE
    own, left, right = take(0), spread(take(1), 1), spread(take(3), 3)
    far_low = spread(far[:split], 2)

    def add(values):
        return jnp.sum(values.astype(F32), axis=0).astype(BF16)

    rows = add(swap(here.reshape(8, 16, 2 * width), ROWS))
    rows = add(swap(jnp.broadcast_to(rows[None], (8, 16, 2 * width)), "zl"))
    rows, left, right, far_low = lax.optimization_barrier((rows, left, right, far_low))
    far_high = spread(far[split:], 2)
    pts = swap(jnp.broadcast_to(rows[None], (32, 16, 2 * width)), ROWS + ("x",))

    def cross(values):
        return lax.ppermute(values, "zh", [(0, 1), (1, 0)])

    def full(rows, dtype=F32, lanes=2 * PANEL):
        return jax.ShapeDtypeStruct((rows, lanes), dtype)

    panel = ((lax.axis_index("zl") >= 4) == (zh_rank == 1)).astype(jnp.int32)
    ranks = jnp.stack([x_rank, zh_rank, panel]).astype(jnp.int32)
    blocks = (own, left, right, far_low, far_high)
    outs = (full(CELLS + 16, BF16), full(CELLS + 16, BF16))
    up, down = whole_call(sums_kernel, outs, [pltpu.VMEM((CELLS, 4 * PANEL), F32)], (ranks,), pts, *blocks)
    ring = [(z % 8) * 2 + z // 8 for z in range(16)]
    below = lax.ppermute(up, ("zl", "zh"), [(ring[z], ring[(z + 4) % 16]) for z in range(16)])
    above = lax.ppermute(down, ("zl", "zh"), [(ring[z], ring[(z + 12) % 16]) for z in range(16)])
    pts, up = lax.optimization_barrier((pts, up))
    gram, other_gram = whole_call(gram_kernel, (full(PANEL), full(PANEL)), [], (ranks,), pts)
    other_gram = cross(other_gram)

    basis_a = real_basis().reshape(16, 5, N).transpose(1, 0, 2).reshape(N, N)
    fields = whole_call(first_kernel, full(16 * 80), [], (), below, above, two_parts(basis_a))
    fields, gram, other_gram = lax.optimization_barrier((fields, gram, other_gram))
    inverse = whole_call(inverse_kernel, full(2 * PANEL), [], (), gram, other_gram)
    fields = swap(fields.reshape(16, 80, 2 * PANEL), PLANE)
    scratch = [pltpu.VMEM((1120, 2 * PANEL), F32), pltpu.VMEM((1280, 2 * PANEL), F32)]
    fields = whole_call(second_kernel, full(1280, BF16), scratch, (), fields, two_parts(second_table()), inverse)
    fields = swap(fields.reshape(32, 40, 2 * PANEL), RING)

    slot = lax.axis_index(RING) * 7 + jnp.arange(7, dtype=jnp.int32)
    square_a = freq_square(lax.axis_index(PLANE) * 5 + slot // 40)
    square_c = freq_square(slot[:, None] % 40 + jnp.arange(2, dtype=jnp.int32)[None, :] * 40)
    square_b = freq_square(jnp.arange(N, dtype=jnp.int32))
    squared = square_a[:, None, None] + square_b[None, :, None] + square_c[:, None, :]
    live = (squared > 0) & (slot < 200)[:, None, None]
    kernel = jnp.where(live, 32.0 * FOUR_PI / jnp.where(squared > 0, squared, 1.0), 0.0)
    kernel = jnp.broadcast_to(kernel[..., None], (7, N, 2, PANEL)).reshape(7 * N, 2 * PANEL)
    part = whole_call(third_kernel, full(PANEL, F32, PANEL), [], (), fields, two_parts(third_table()), kernel)
    part = part.reshape(2, 4, 8, PANEL).transpose(1, 0, 2, 3)
    part = jnp.broadcast_to(part[None], (8, 4, 2, 8, PANEL)).reshape(32, 16, PANEL)
    part = jnp.sum(swap(part, ROWS + ("x",)), axis=0)
    part = jnp.broadcast_to(part.reshape(1, 2, 8, PANEL), (8, 2, 8, PANEL)).reshape(16, 8, PANEL)
    return jnp.sum(swap(part, ("zl", "zh")), axis=0)


def solution(mesh):
    devices = mesh.devices.reshape(8, 2, 2, 2, 2, 4)
    inner = Mesh(devices, ("zl", "yh", "yl", "c", "zh", "x"))
    in_specs = (P(None, GRID, ORB), P(None, GRID, ORB), P(), P())
    return jax.shard_map(shards, mesh=inner, in_specs=in_specs, out_specs=P(ORB, None), check_vma=False)
```

```python
import math

import jax
import jax.numpy as jnp
import ml_dtypes
import numpy as np
from jax import lax
from jax.experimental import pallas as pl
from jax.experimental.pallas import tpu as pltpu
from jax.sharding import Mesh, PartitionSpec as P

N = 80
PANEL = 64
GRID = ("zl", "yh", "yl", "c")
ORB = ("zh", "x")
ROWS = ("yh", "yl", "c")
PLANE = ("yl", "c", "x")
RING = ("yh", "zl", "zh")
BF16 = jnp.bfloat16
F32 = jnp.float32
LEVELS = 252.9
SPAN = 5.21
SHIFTS = (0, 1, 3, 2)
ROWS_A = 1280
ROWS_B = 720
FOUR_PI = 4.0 * math.pi
TWO_PI = 2.0 * math.pi


def real_basis():
    steps = np.arange(N)
    freqs = np.concatenate([np.arange(N // 2 + 1), np.arange(1, N // 2)])
    angle = TWO_PI / N * (freqs[:, None] * steps[None, :] % N)
    table = np.where(np.arange(N)[:, None] <= N // 2, np.cos(angle), np.sin(angle)) * math.sqrt(2.0 / N)
    table[0] /= math.sqrt(2.0)
    table[N // 2] /= math.sqrt(2.0)
    return table.astype(np.float32)


def freq_square(index):
    freq = jnp.where(index > N // 2, index - N // 2, index).astype(F32)
    wave = TWO_PI / N * freq
    return wave * wave


def mix(form, left, right):
    return jnp.einsum(form, left, right, precision=lax.Precision.HIGHEST, preferred_element_type=F32)


def swap(values, axes):
    return lax.all_to_all(values, axes, 0, 0, tiled=True)


def lane_power(square_sum, count):
    return jnp.ceil(0.5 * jnp.log2(jnp.maximum(square_sum * (1.0 / count), 1e-37))) - 1.0


def encode(values, power):
    size = jnp.abs(values) * jnp.exp2(-power)
    level = jnp.log(size + jnp.sqrt(size * size + 1.0)) * (LEVELS / SPAN)
    whole = jnp.floor(level)
    code = jnp.exp2(whole - 126.0) * (1.0 + (level - whole))
    return jnp.where(values < 0, -code, code)


def decode(code, power):
    size = jnp.abs(code)
    whole = jnp.floor(jnp.log2(size) + 1e-3)
    level = whole + (size * jnp.exp2(-whole) - 1.0) + 126.0
    spread = jnp.exp(level * (SPAN / LEVELS))
    value = 0.5 * (spread - 1.0 / spread) * jnp.exp2(power)
    return jnp.where(code < 0, -value, value)


def whole_call(kernel, out_shape, scratch, scalars, *arrays, flops=2 * 10**9):
    vmem = pl.BlockSpec(memory_space=pltpu.VMEM)
    shapes = [a.shape for a in arrays]
    moved = sum(math.prod(shape) * 4 for shape in shapes)
    return pl.pallas_call(
        kernel,
        out_shape=out_shape,
        in_specs=[pl.BlockSpec(memory_space=pltpu.SMEM)] * len(scalars) + [vmem] * len(arrays),
        out_specs=jax.tree.map(lambda _: vmem, out_shape),
        scratch_shapes=scratch,
        compiler_params=pltpu.CompilerParams(vmem_limit_bytes=40 * 2**20),
        cost_estimate=pl.CostEstimate(flops=flops, bytes_accessed=moved, transcendentals=0),
    )(*scalars, *arrays)


def head_rows(points_ref, shift, x_rank, panel):
    block = lax.rem(x_rank - shift + 4, 4)
    return jnp.concatenate([points_ref[(panel * 4 + i) * 4 + block] for i in range(4)], axis=0)


def side_table(head):
    half = head.shape[1] // 2
    gap = jnp.zeros((head.shape[0], half), head.dtype)
    upper = jnp.concatenate([head[:, :half], gap], axis=1)
    lower = jnp.concatenate([gap, head[:, half:]], axis=1)
    return jnp.concatenate([upper, lower], axis=0)


def dot_rows(left, right, precision=None):
    return lax.dot_general(left, right, (((1,), (1,)), ((), ())), precision=precision, preferred_element_type=F32)


def split(values):
    high = values.astype(BF16)
    return high, (values - high.astype(F32)).astype(BF16)


def dot_two(table_ref, values):
    high, low = split(values)
    count = table_ref.shape[0] // 2
    top, rest = table_ref[pl.ds(0, count), :], table_ref[pl.ds(count, count), :]
    return dot(top, high) + (dot(top, low) + dot(rest, high))


def dot(left, right):
    return lax.dot_general(left, right, (((1,), (0,)), ((), ())), preferred_element_type=F32)


def dot_three(left, right):
    (left, left_rest), (right, right_rest) = split(left), split(right)
    return dot(left, right) + (dot(left, right_rest) + dot(left_rest, right))


def two_parts(table):
    high = table.astype(ml_dtypes.bfloat16)
    low = (table - high.astype(np.float32)).astype(ml_dtypes.bfloat16)
    return jnp.asarray(np.concatenate([high, low], axis=0))


def sums_kernel(rank_ref, points_ref, own, left, right, far, one_ref, two_ref, sum_ref):
    panel_one = rank_ref[1]
    count = own.shape[0]
    tables = []
    for shift in SHIFTS:
        heads = [head_rows(points_ref, shift, rank_ref[0], panel) for panel in (panel_one, 1 - panel_one)]
        tables.append(jnp.concatenate([side_table(head) for head in heads], axis=0))
    tile = 320 if count == ROWS_A else 240
    tiles = [pl.ds(low, tile) for low in range(0, count, tile)]
    square = jnp.zeros((1, 4 * PANEL), F32)
    for rows in tiles:
        total = sum(dot_rows(block[rows, :], table) for block, table in zip((own, left, right, far), tables))
        sum_ref[rows, :] = total
        square = square + jnp.sum(total * total, axis=0, keepdims=True)
    power = lane_power(square, count)
    for out_ref, low in ((one_ref, 0), (two_ref, 2 * PANEL)):
        lanes = pl.ds(low, 2 * PANEL)
        own_power = power[:, low : low + 2 * PANEL]
        for rows in tiles:
            out_ref[rows, :] = encode(sum_ref[rows, lanes], own_power).astype(BF16)
        out_ref[pl.ds(count, 16), :] = jnp.broadcast_to(own_power, (16, 2 * PANEL)).astype(BF16)


def gram_kernel(rank_ref, points_ref, gram_ref):
    for panel in range(2):
        heads = [head_rows(points_ref, shift, rank_ref[0], panel) for shift in SHIFTS]
        gram_ref[pl.ds(panel * PANEL, PANEL), :] = sum(dot_rows(head, side_table(head)) for head in heads)


def first_kernel(below_a, above_a, below_b, above_b, basis_ref, out_ref):
    left_lanes = lax.broadcasted_iota(jnp.int32, (N, 2 * PANEL), 1) < PANEL
    out_ref[...] = jnp.zeros_like(out_ref)

    def product(column):
        refs, count = ((below_a, above_a), ROWS_A) if column < ROWS_A // N else ((below_b, above_b), ROWS_B)
        rows = pl.ds(column * N % ROWS_A, N)
        parts = [decode(ref[rows, :].astype(F32), ref[pl.ds(count, 16), :].astype(F32)[:1]) for ref in refs]
        sums = parts[0] + parts[1]
        return sums * pltpu.roll(sums, PANEL, 1)

    pairs = []
    for pair in range(13):
        right = product(pair + 13) if pair < 12 else 0.0
        pairs.append(jnp.where(left_lanes, product(pair), right))
    moved = dot_two(basis_ref, jnp.concatenate(pairs, axis=1))
    for pair in range(13):
        for k in range(5):
            rows = moved[k * 16 : k * 16 + 16, pair * 2 * PANEL : (pair + 1) * 2 * PANEL]
            out_ref[pl.ds(k * 16 + pair, 16, stride=80), :] = rows


def inverse_kernel(mine_ref, other_ref, fit_ref, bra_ref):
    sums = mine_ref[...] + other_ref[...]
    both = sums * pltpu.roll(sums, PANEL, 1)
    lane = lax.broadcasted_iota(jnp.int32, (PANEL, 2 * PANEL), 1)
    line = lax.broadcasted_iota(jnp.int32, (PANEL, 2 * PANEL), 0)
    left = lane < PANEL
    matrix = jnp.where(left, both[:PANEL], both[PANEL:])
    for step in range(PANEL):
        far = PANEL + step
        here = (lane == step) | (lane == far)
        row = matrix[step : step + 1]
        pivot = jnp.where(left[:1], row[:, step : step + 1], row[:, far : far + 1])
        row = jnp.where(here[:1], 1.0, row) / pivot
        column = jnp.where(left, matrix[:, step : step + 1], matrix[:, far : far + 1])
        rest = jnp.where(here, 0.0, matrix) - column * row
        matrix = jnp.where(line == step, row, rest)
    other = pltpu.roll(matrix, PANEL, 1)
    fit_ref[...] = jnp.where(left, matrix, other)
    bra_ref[...] = jnp.where(left, other, matrix)


def second_kernel(in_ref, table_ref, out_ref, line_ref, code_ref):
    left_lanes = lax.broadcasted_iota(jnp.int32, (200, 2 * PANEL), 1) < PANEL
    data = [in_ref[:, pl.ds(k * 16, 16), :].reshape(256, 2 * PANEL) for k in range(5)]
    moved = dot_two(table_ref, jnp.concatenate(data, axis=1))
    square = jnp.zeros((1, 2 * PANEL), F32)
    for k in range(5):
        part = moved[:, k * 2 * PANEL : (k + 1) * 2 * PANEL]
        low = part[:200] + pltpu.roll(part[200:400], PANEL, 1)
        high = pltpu.roll(part[400:600], PANEL, 1) + part[600:]
        mixed = jnp.where(left_lanes, low, high)
        line_ref[pl.ds(k * 200, 200), :] = mixed
        square = square + jnp.sum(mixed * mixed, axis=0, keepdims=True)
    power = lane_power(square, 1000)
    line_ref[pl.ds(1000, 120), :] = jnp.zeros((120, 2 * PANEL), F32)
    for tile in range(4):
        rows = pl.ds(tile * 280, 280)
        line_ref[rows, :] = encode(line_ref[rows, :], power)
    for to in range(32):
        code_ref[pl.ds(40 * to, 35), :] = line_ref[pl.ds(35 * to, 35), :]
        code_ref[pl.ds(40 * to + 35, 5), :] = jnp.broadcast_to(power, (5, 2 * PANEL))
    for tile in range(4):
        rows = pl.ds(tile * 320, 320)
        out_ref[rows, :] = code_ref[rows, :].astype(BF16)


def third_kernel(got_ref, table_ref, kernel_ref, fit_ref, bra_ref, out_ref):
    keep = lax.broadcasted_iota(jnp.int32, (40, 2 * PANEL), 0) < 35

    def side(panel):
        parts = []
        for source in range(16):
            block = got_ref[2 * source + (panel + (source % 8 < 4)) % 2].astype(F32)
            parts.append(jnp.where(keep, decode(jnp.where(keep, block, 1.0), block[35:36]), 0.0))
        return jnp.concatenate(parts, axis=0)

    moved = dot_two(table_ref, jnp.concatenate([side(0), side(1)], axis=1))
    fit_top, fit_rest = split(moved[:, : 2 * PANEL] * kernel_ref[...])
    bra_top, bra_rest = split(moved[:, 2 * PANEL :])

    def meet(left, right):
        return lax.dot_general(left, right, (((0,), (0,)), ((), ())), preferred_element_type=F32)

    total = meet(bra_top, fit_top) + (meet(bra_top, fit_rest) + meet(bra_rest, fit_top))
    total = total + pltpu.roll(pltpu.roll(total, PANEL, 0), PANEL, 1)
    total = dot_three(bra_ref[...][:, :PANEL], total[:PANEL, :PANEL])
    total = dot_three(total, fit_ref[...])
    left_lanes = lax.broadcasted_iota(jnp.int32, (8, 2 * PANEL), 1) < PANEL
    for to in range(4):
        rows = jnp.where(left_lanes, total[8 * to : 8 * to + 8], total[32 + 8 * to : 40 + 8 * to])
        for row in range(8):
            out_ref[row * 4 + to] = rows


def second_table():
    basis = real_basis().astype(np.float64)
    full = np.zeros((N, 5, 5 * N))
    for row in range(5):
        full[:, row, row * N : (row + 1) * N] = basis
    full = full.reshape(2, 200, 16, 25)
    table = np.zeros((2, 2, 200, 16, 16))
    table[:, 0, :, :, :13] = full[..., :13]
    table[:, 1, :, :, :12] = full[..., 13:]
    return table.reshape(800, 256).astype(np.float32)


def third_table():
    basis = np.roll(real_basis().reshape(N, 8, 2, 5).transpose(0, 2, 1, 3), 4, axis=2)
    table = np.zeros((7, N, 2, 8, 40), np.float32)
    for pair in range(7):
        table[pair, ..., pair * 5 : pair * 5 + 5] = basis
    return table.reshape(7 * N, 640)


def shards(occupied, virtual, points, panels):
    x_rank = lax.axis_index("x")
    zh_rank = lax.axis_index("zh")
    grid_rank = lax.axis_index(GRID)
    columns = occupied.shape[1]
    width = occupied.shape[2]
    per_x = columns // 4

    parts = jnp.concatenate([occupied, virtual], axis=2).reshape(N, 4, per_x, 2 * width)
    parts = parts.transpose(1, 2, 0, 3).reshape(4, per_x * N, 2 * width)

    wanted = panels.reshape(-1, 1) == jnp.arange(2 * PANEL, dtype=jnp.int32)
    chosen = jnp.sum(jnp.where(wanted, points, 0), axis=1)
    within = chosen % (N * N) - grid_rank * columns
    inside = (within >= 0) & (within < columns)
    plane_of = chosen // (N * N)
    column_of = jnp.where(inside, within, 0)
    here = jnp.concatenate([occupied[plane_of, column_of], virtual[plane_of, column_of]], axis=1)
    here = jnp.where(inside[:, None], here, jnp.zeros((), BF16))

    def take(shift):
        return lax.dynamic_index_in_dim(parts, (x_rank + shift) % 4, 0, keepdims=False)

    def spread(block, shift):
        return lax.ppermute(block, "x", [(i, (i + shift) % 4) for i in range(4)])

    whole = [take(shift) for shift in SHIFTS]
    first = [block[:ROWS_A] for block in whole]
    second = [block[ROWS_A:] for block in whole]
    first = first[:1] + [spread(block, shift) for block, shift in zip(first[1:], SHIFTS[1:])]

    def add(values):
        return jnp.sum(values.astype(F32), axis=0).astype(BF16)

    rows = add(swap(here.reshape(8, 16, 2 * width), ROWS))
    rows = add(swap(jnp.broadcast_to(rows[None], (8, 16, 2 * width)), "zl"))
    rows, first = lax.optimization_barrier((rows, first))
    pts = swap(jnp.broadcast_to(rows[None], (32, 16, 2 * width)), ROWS + ("x",))
    pts, second = lax.optimization_barrier((pts, second))
    second = second[:1] + [spread(block, shift) for block, shift in zip(second[1:], SHIFTS[1:])]

    def cross(values):
        return lax.ppermute(values, "zh", [(0, 1), (1, 0)])

    def full(rows, dtype=F32, lanes=2 * PANEL):
        return jax.ShapeDtypeStruct((rows, lanes), dtype)

    ranks = jnp.stack([x_rank, (zh_rank + lax.axis_index("c")) % 2]).astype(jnp.int32)

    def hops(core_zero):
        pairs = []
        for z in range(16):
            for core, step in ((0, core_zero), (1, 16 - core_zero)):
                to = (z + step) % 16
                pairs.append((((z % 8) * 2 + core) * 2 + z // 8, ((to % 8) * 2 + core) * 2 + to // 8))
        return pairs

    def half_sums(points, blocks):
        count = blocks[0].shape[0]
        outs = (full(count + 16, BF16), full(count + 16, BF16))
        scratch = [pltpu.VMEM((count, 4 * PANEL), F32)]
        one, two = whole_call(sums_kernel, outs, scratch, (ranks,), points, *blocks)
        return one, lax.ppermute(one, ("zl", "c", "zh"), hops(4)), lax.ppermute(two, ("zl", "c", "zh"), hops(12))

    one, *got_a = half_sums(pts, first)
    _, *got_b = half_sums(pts, second)
    pts, one = lax.optimization_barrier((pts, one))
    gram = whole_call(gram_kernel, full(2 * PANEL), [], (ranks,), pts, flops=0)
    other_gram = cross(gram)

    basis_a = real_basis().reshape(16, 5, N).transpose(1, 0, 2).reshape(N, N)
    fields = whole_call(first_kernel, full(16 * 80), [], (), *got_a, *got_b, two_parts(basis_a))
    fields = swap(fields.reshape(16, 80, 2 * PANEL), PLANE)
    scratch = [pltpu.VMEM((1120, 2 * PANEL), F32), pltpu.VMEM((1280, 2 * PANEL), F32)]
    fields = whole_call(second_kernel, full(1280, BF16), scratch, (), fields, two_parts(second_table()))
    fields, gram, other_gram = lax.optimization_barrier((fields, gram, other_gram))
    inverses = whole_call(inverse_kernel, (full(PANEL), full(PANEL)), [], (), gram, other_gram)
    fields = swap(fields.reshape(32, 40, 2 * PANEL), RING)

    slot = lax.axis_index(RING) * 7 + jnp.arange(7, dtype=jnp.int32)
    square_a = freq_square(lax.axis_index(PLANE) * 5 + slot // 40)
    square_c = freq_square(slot[:, None] % 40 + jnp.arange(2, dtype=jnp.int32)[None, :] * 40)
    square_b = freq_square(jnp.arange(N, dtype=jnp.int32))
    squared = square_a[:, None, None] + square_b[None, :, None] + square_c[:, None, :]
    live = (squared > 0) & (slot < 200)[:, None, None]
    kernel = jnp.where(live, 32.0 * FOUR_PI / jnp.where(squared > 0, squared, 1.0), 0.0)
    kernel = jnp.broadcast_to(kernel[..., None], (7, N, 2, PANEL)).reshape(7 * N, 2 * PANEL)
    out_shape = jax.ShapeDtypeStruct((32, 8, 2 * PANEL), F32)
    part = whole_call(third_kernel, out_shape, [], (), fields, two_parts(third_table()), kernel, *inverses)
    part = jnp.sum(swap(part, ROWS + ("x",)), axis=0)
    part = jnp.sum(swap(jnp.broadcast_to(part[None], (16, 8, 2 * PANEL)), ("zl", "zh")), axis=0)
    return lax.dynamic_slice_in_dim(part, zh_rank * PANEL, PANEL, 1)


def solution(mesh):
    devices = mesh.devices.reshape(8, 2, 2, 2, 2, 4)
    inner = Mesh(devices, ("zl", "yh", "yl", "c", "zh", "x"))
    in_specs = (P(None, GRID, ORB), P(None, GRID, ORB), P(), P())
    return jax.shard_map(shards, mesh=inner, in_specs=in_specs, out_specs=P(ORB, None), check_vma=False)
```

```python
import math

import jax
import jax.numpy as jnp
import ml_dtypes
import numpy as np
from jax import lax
from jax.experimental import pallas as pl
from jax.experimental.pallas import tpu as pltpu
from jax.sharding import Mesh, PartitionSpec as P

N = 80
PANEL = 64
GRID = ("zl", "yh", "yl", "c")
ORB = ("zh", "x")
ROWS = ("yh", "yl", "c")
PLANE = ("yl", "c", "x")
RING = ("yh", "zl", "zh")
BF16 = jnp.bfloat16
F32 = jnp.float32
LEVELS = 252.9
SPAN = 5.21
SHIFTS = (0, 1, 3, 2)
ROWS_A = 1280
ROWS_B = 720
FOUR_PI = 4.0 * math.pi
TWO_PI = 2.0 * math.pi


def real_basis():
    steps = np.arange(N)
    freqs = np.concatenate([np.arange(N // 2 + 1), np.arange(1, N // 2)])
    angle = TWO_PI / N * (freqs[:, None] * steps[None, :] % N)
    table = np.where(np.arange(N)[:, None] <= N // 2, np.cos(angle), np.sin(angle)) * math.sqrt(2.0 / N)
    table[0] /= math.sqrt(2.0)
    table[N // 2] /= math.sqrt(2.0)
    return table.astype(np.float32)


def freq_square(index):
    freq = jnp.where(index > N // 2, index - N // 2, index).astype(F32)
    wave = TWO_PI / N * freq
    return wave * wave


def mix(form, left, right):
    return jnp.einsum(form, left, right, precision=lax.Precision.HIGHEST, preferred_element_type=F32)


def swap(values, axes):
    return lax.all_to_all(values, axes, 0, 0, tiled=True)


def lane_power(square_sum, count):
    return jnp.ceil(0.5 * jnp.log2(jnp.maximum(square_sum * (1.0 / count), 1e-37))) - 1.0


def encode(values, power):
    size = jnp.abs(values) * jnp.exp2(-power)
    level = jnp.log(size + jnp.sqrt(size * size + 1.0)) * (LEVELS / SPAN)
    whole = jnp.floor(level)
    code = jnp.exp2(whole - 126.0) * (1.0 + (level - whole))
    return jnp.where(values < 0, -code, code)


def decode(code, power):
    size = jnp.abs(code)
    whole = jnp.floor(jnp.log2(size) + 1e-3)
    level = whole + (size * jnp.exp2(-whole) - 1.0) + 126.0
    spread = jnp.exp(level * (SPAN / LEVELS))
    value = 0.5 * (spread - 1.0 / spread) * jnp.exp2(power)
    return jnp.where(code < 0, -value, value)


def whole_call(kernel, out_shape, scratch, scalars, *arrays, flops=2 * 10**9):
    vmem = pl.BlockSpec(memory_space=pltpu.VMEM)
    shapes = [a.shape for a in arrays]
    moved = sum(math.prod(shape) * 4 for shape in shapes)
    return pl.pallas_call(
        kernel,
        out_shape=out_shape,
        in_specs=[pl.BlockSpec(memory_space=pltpu.SMEM)] * len(scalars) + [vmem] * len(arrays),
        out_specs=jax.tree.map(lambda _: vmem, out_shape),
        scratch_shapes=scratch,
        compiler_params=pltpu.CompilerParams(vmem_limit_bytes=40 * 2**20),
        cost_estimate=pl.CostEstimate(flops=flops, bytes_accessed=moved, transcendentals=0),
    )(*scalars, *arrays)


def head_rows(points_ref, shift, x_rank, panel):
    block = lax.rem(x_rank - shift + 4, 4)
    return jnp.concatenate([points_ref[(panel * 4 + i) * 4 + block] for i in range(4)], axis=0)


def side_table(head):
    half = head.shape[1] // 2
    gap = jnp.zeros((head.shape[0], half), head.dtype)
    upper = jnp.concatenate([head[:, :half], gap], axis=1)
    lower = jnp.concatenate([gap, head[:, half:]], axis=1)
    return jnp.concatenate([upper, lower], axis=0)


def dot_rows(left, right, precision=None):
    return lax.dot_general(left, right, (((1,), (1,)), ((), ())), precision=precision, preferred_element_type=F32)


def split(values):
    high = values.astype(BF16)
    return high, (values - high.astype(F32)).astype(BF16)


def dot_two(table_ref, values):
    high, low = split(values)
    count = table_ref.shape[0] // 2
    top, rest = table_ref[pl.ds(0, count), :], table_ref[pl.ds(count, count), :]
    return dot(top, high) + (dot(top, low) + dot(rest, high))


def dot(left, right):
    return lax.dot_general(left, right, (((1,), (0,)), ((), ())), preferred_element_type=F32)


def dot_three(left, right):
    (left, left_rest), (right, right_rest) = split(left), split(right)
    return dot(left, right) + (dot(left, right_rest) + dot(left_rest, right))


def two_parts(table):
    high = table.astype(ml_dtypes.bfloat16)
    low = (table - high.astype(np.float32)).astype(ml_dtypes.bfloat16)
    return jnp.asarray(np.concatenate([high, low], axis=0))


def sums_kernel(rank_ref, points_ref, own, left, right, far, one_ref, two_ref, sum_ref):
    panel_one = rank_ref[1]
    count = own.shape[0]
    tables = []
    for shift in SHIFTS:
        heads = [head_rows(points_ref, shift, rank_ref[0], panel) for panel in (panel_one, 1 - panel_one)]
        tables.append(jnp.concatenate([side_table(head) for head in heads], axis=0))
    tile = 320 if count == ROWS_A else 240
    tiles = [pl.ds(low, tile) for low in range(0, count, tile)]
    square = jnp.zeros((1, 4 * PANEL), F32)
    for rows in tiles:
        total = sum(dot_rows(block[rows, :], table) for block, table in zip((own, left, right, far), tables))
        sum_ref[rows, :] = total
        square = square + jnp.sum(total * total, axis=0, keepdims=True)
    power = lane_power(square, count)
    for out_ref, low in ((one_ref, 0), (two_ref, 2 * PANEL)):
        lanes = pl.ds(low, 2 * PANEL)
        own_power = power[:, low : low + 2 * PANEL]
        for rows in tiles:
            out_ref[rows, :] = encode(sum_ref[rows, lanes], own_power).astype(BF16)
        out_ref[pl.ds(count, 16), :] = jnp.broadcast_to(own_power, (16, 2 * PANEL)).astype(BF16)


def gram_kernel(rank_ref, points_ref, gram_ref):
    for panel in range(2):
        heads = [head_rows(points_ref, shift, rank_ref[0], panel) for shift in SHIFTS]
        gram_ref[pl.ds(panel * PANEL, PANEL), :] = sum(dot_rows(head, side_table(head)) for head in heads)


def first_kernel(below_a, above_a, below_b, above_b, basis_ref, out_ref):
    left_lanes = lax.broadcasted_iota(jnp.int32, (N, 2 * PANEL), 1) < PANEL
    out_ref[...] = jnp.zeros_like(out_ref)

    def product(column):
        refs, count = ((below_a, above_a), ROWS_A) if column < ROWS_A // N else ((below_b, above_b), ROWS_B)
        rows = pl.ds(column * N % ROWS_A, N)
        parts = [decode(ref[rows, :].astype(F32), ref[pl.ds(count, 16), :].astype(F32)[:1]) for ref in refs]
        sums = parts[0] + parts[1]
        return sums * pltpu.roll(sums, PANEL, 1)

    pairs = []
    for pair in range(13):
        right = product(pair + 13) if pair < 12 else 0.0
        pairs.append(jnp.where(left_lanes, product(pair), right))
    moved = dot_two(basis_ref, jnp.concatenate(pairs, axis=1))
    for pair in range(13):
        for k in range(5):
            rows = moved[k * 16 : k * 16 + 16, pair * 2 * PANEL : (pair + 1) * 2 * PANEL]
            out_ref[pl.ds(k * 16 + pair, 16, stride=80), :] = rows


def inverse_kernel(mine_ref, other_ref, fit_ref, bra_ref):
    sums = mine_ref[...] + other_ref[...]
    both = sums * pltpu.roll(sums, PANEL, 1)
    lane = lax.broadcasted_iota(jnp.int32, (PANEL, 2 * PANEL), 1)
    line = lax.broadcasted_iota(jnp.int32, (PANEL, 2 * PANEL), 0)
    left = lane < PANEL
    matrix = jnp.where(left, both[:PANEL], both[PANEL:])
    for step in range(PANEL):
        far = PANEL + step
        here = (lane == step) | (lane == far)
        row = matrix[step : step + 1]
        pivot = jnp.where(left[:1], row[:, step : step + 1], row[:, far : far + 1])
        row = jnp.where(here[:1], 1.0, row) / pivot
        column = jnp.where(left, matrix[:, step : step + 1], matrix[:, far : far + 1])
        rest = jnp.where(here, 0.0, matrix) - column * row
        matrix = jnp.where(line == step, row, rest)
    other = pltpu.roll(matrix, PANEL, 1)
    fit_ref[...] = jnp.where(left, matrix, other)
    bra_ref[...] = jnp.where(left, other, matrix)


def second_kernel(in_ref, table_ref, out_ref, line_ref, code_ref):
    left_lanes = lax.broadcasted_iota(jnp.int32, (200, 2 * PANEL), 1) < PANEL
    data = [in_ref[:, pl.ds(k * 16, 16), :].reshape(256, 2 * PANEL) for k in range(5)]
    moved = dot_two(table_ref, jnp.concatenate(data, axis=1))
    square = jnp.zeros((1, 2 * PANEL), F32)
    for k in range(5):
        part = moved[:, k * 2 * PANEL : (k + 1) * 2 * PANEL]
        low = part[:200] + pltpu.roll(part[200:400], PANEL, 1)
        high = pltpu.roll(part[400:600], PANEL, 1) + part[600:]
        mixed = jnp.where(left_lanes, low, high)
        line_ref[pl.ds(k * 200, 200), :] = mixed
        square = square + jnp.sum(mixed * mixed, axis=0, keepdims=True)
    power = lane_power(square, 1000)
    line_ref[pl.ds(1000, 120), :] = jnp.zeros((120, 2 * PANEL), F32)
    for tile in range(4):
        rows = pl.ds(tile * 280, 280)
        line_ref[rows, :] = encode(line_ref[rows, :], power)
    for to in range(32):
        code_ref[pl.ds(40 * to, 35), :] = line_ref[pl.ds(35 * to, 35), :]
        code_ref[pl.ds(40 * to + 35, 5), :] = jnp.broadcast_to(power, (5, 2 * PANEL))
    for tile in range(4):
        rows = pl.ds(tile * 320, 320)
        out_ref[rows, :] = code_ref[rows, :].astype(BF16)


def third_kernel(got_ref, table_ref, kernel_ref, fit_ref, bra_ref, out_ref):
    keep = lax.broadcasted_iota(jnp.int32, (40, 2 * PANEL), 0) < 35

    def side(panel):
        parts = []
        for source in range(16):
            block = got_ref[2 * source + (panel + (source % 8 < 4)) % 2].astype(F32)
            parts.append(jnp.where(keep, decode(jnp.where(keep, block, 1.0), block[35:36]), 0.0))
        return jnp.concatenate(parts, axis=0)

    moved = dot_two(table_ref, jnp.concatenate([side(0), side(1)], axis=1))
    fit_top, fit_rest = split(moved[:, : 2 * PANEL] * kernel_ref[...])
    bra_top, bra_rest = split(moved[:, 2 * PANEL :])

    def meet(left, right):
        return lax.dot_general(left, right, (((0,), (0,)), ((), ())), preferred_element_type=F32)

    total = meet(bra_top, fit_top) + (meet(bra_top, fit_rest) + meet(bra_rest, fit_top))
    total = total + pltpu.roll(pltpu.roll(total, PANEL, 0), PANEL, 1)
    total = dot_three(bra_ref[...][:, :PANEL], total[:PANEL, :PANEL])
    total = dot_three(total, fit_ref[...])
    left_lanes = lax.broadcasted_iota(jnp.int32, (8, 2 * PANEL), 1) < PANEL
    for to in range(4):
        rows = jnp.where(left_lanes, total[8 * to : 8 * to + 8], total[32 + 8 * to : 40 + 8 * to])
        for row in range(8):
            out_ref[row * 4 + to] = rows


def second_table():
    basis = real_basis().astype(np.float64)
    full = np.zeros((N, 5, 5 * N))
    for row in range(5):
        full[:, row, row * N : (row + 1) * N] = basis
    full = full.reshape(2, 200, 16, 25)
    table = np.zeros((2, 2, 200, 16, 16))
    table[:, 0, :, :, :13] = full[..., :13]
    table[:, 1, :, :, :12] = full[..., 13:]
    return table.reshape(800, 256).astype(np.float32)


def third_table():
    basis = np.roll(real_basis().reshape(N, 8, 2, 5).transpose(0, 2, 1, 3), 4, axis=2)
    table = np.zeros((7, N, 2, 8, 40), np.float32)
    for pair in range(7):
        table[pair, ..., pair * 5 : pair * 5 + 5] = basis
    return table.reshape(7 * N, 640)


def shards(occupied, virtual, points, panels):
    x_rank = lax.axis_index("x")
    zh_rank = lax.axis_index("zh")
    grid_rank = lax.axis_index(GRID)
    columns = occupied.shape[1]
    width = occupied.shape[2]
    per_x = columns // 4

    parts = jnp.concatenate([occupied, virtual], axis=2).reshape(N, 4, per_x, 2 * width)
    parts = parts.transpose(1, 2, 0, 3).reshape(4, per_x * N, 2 * width)

    wanted = panels.reshape(-1, 1) == jnp.arange(2 * PANEL, dtype=jnp.int32)
    chosen = jnp.sum(jnp.where(wanted, points, 0), axis=1)
    within = chosen % (N * N) - grid_rank * columns
    inside = (within >= 0) & (within < columns)
    plane_of = chosen // (N * N)
    column_of = jnp.where(inside, within, 0)
    here = jnp.concatenate([occupied[plane_of, column_of], virtual[plane_of, column_of]], axis=1)
    here = jnp.where(inside[:, None], here, jnp.zeros((), BF16))

    def take(shift):
        return lax.dynamic_index_in_dim(parts, (x_rank + shift) % 4, 0, keepdims=False)

    def spread(block, shift):
        return lax.ppermute(block, "x", [(i, (i + shift) % 4) for i in range(4)])

    whole = [take(shift) for shift in SHIFTS]
    first = [block[:ROWS_A] for block in whole]
    second = [block[ROWS_A:] for block in whole]
    first = first[:1] + [spread(block, shift) for block, shift in zip(first[1:], SHIFTS[1:])]

    def add(values):
        return jnp.sum(values.astype(F32), axis=0).astype(BF16)

    rows = add(swap(here.reshape(8, 16, 2 * width), ROWS))
    rows = add(swap(jnp.broadcast_to(rows[None], (8, 16, 2 * width)), "zl"))
    rows, first = lax.optimization_barrier((rows, first))
    pts = swap(jnp.broadcast_to(rows[None], (32, 16, 2 * width)), ROWS + ("x",))
    second = second[:1] + [spread(block, shift) for block, shift in zip(second[1:], SHIFTS[1:])]

    def cross(values):
        return lax.ppermute(values, "zh", [(0, 1), (1, 0)])

    def full(rows, dtype=F32, lanes=2 * PANEL):
        return jax.ShapeDtypeStruct((rows, lanes), dtype)

    ranks = jnp.stack([x_rank, (zh_rank + lax.axis_index("c")) % 2]).astype(jnp.int32)

    def hops(core_zero):
        pairs = []
        for z in range(16):
            for core, step in ((0, core_zero), (1, 16 - core_zero)):
                to = (z + step) % 16
                pairs.append((((z % 8) * 2 + core) * 2 + z // 8, ((to % 8) * 2 + core) * 2 + to // 8))
        return pairs

    def half_sums(points, blocks):
        count = blocks[0].shape[0]
        outs = (full(count + 16, BF16), full(count + 16, BF16))
        scratch = [pltpu.VMEM((count, 4 * PANEL), F32)]
        one, two = whole_call(sums_kernel, outs, scratch, (ranks,), points, *blocks)
        return one, lax.ppermute(one, ("zl", "c", "zh"), hops(4)), lax.ppermute(two, ("zl", "c", "zh"), hops(12))

    one, *got_a = half_sums(pts, first)
    _, *got_b = half_sums(pts, second)
    pts, one = lax.optimization_barrier((pts, one))
    gram = whole_call(gram_kernel, full(2 * PANEL), [], (ranks,), pts, flops=0)
    other_gram = cross(gram)

    basis_a = real_basis().reshape(16, 5, N).transpose(1, 0, 2).reshape(N, N)
    fields = whole_call(first_kernel, full(16 * 80), [], (), *got_a, *got_b, two_parts(basis_a))
    fields = swap(fields.reshape(16, 80, 2 * PANEL), PLANE)
    scratch = [pltpu.VMEM((1120, 2 * PANEL), F32), pltpu.VMEM((1280, 2 * PANEL), F32)]
    fields = whole_call(second_kernel, full(1280, BF16), scratch, (), fields, two_parts(second_table()))
    fields, gram, other_gram = lax.optimization_barrier((fields, gram, other_gram))
    inverses = whole_call(inverse_kernel, (full(PANEL), full(PANEL)), [], (), gram, other_gram)
    fields = swap(fields.reshape(32, 40, 2 * PANEL), RING)

    slot = lax.axis_index(RING) * 7 + jnp.arange(7, dtype=jnp.int32)
    square_a = freq_square(lax.axis_index(PLANE) * 5 + slot // 40)
    square_c = freq_square(slot[:, None] % 40 + jnp.arange(2, dtype=jnp.int32)[None, :] * 40)
    square_b = freq_square(jnp.arange(N, dtype=jnp.int32))
    squared = square_a[:, None, None] + square_b[None, :, None] + square_c[:, None, :]
    live = (squared > 0) & (slot < 200)[:, None, None]
    kernel = jnp.where(live, 32.0 * FOUR_PI / jnp.where(squared > 0, squared, 1.0), 0.0)
    kernel = jnp.broadcast_to(kernel[..., None], (7, N, 2, PANEL)).reshape(7 * N, 2 * PANEL)
    out_shape = jax.ShapeDtypeStruct((32, 8, 2 * PANEL), F32)
    part = whole_call(third_kernel, out_shape, [], (), fields, two_parts(third_table()), kernel, *inverses)
    part = jnp.sum(swap(part, ROWS + ("x",)), axis=0)
    part = jnp.sum(swap(jnp.broadcast_to(part[None], (16, 8, 2 * PANEL)), ("zl", "zh")), axis=0)
    return lax.dynamic_slice_in_dim(part, zh_rank * PANEL, PANEL, 1)


def solution(mesh):
    devices = mesh.devices.reshape(8, 2, 2, 2, 2, 4)
    inner = Mesh(devices, ("zl", "yh", "yl", "c", "zh", "x"))
    in_specs = (P(None, GRID, ORB), P(None, GRID, ORB), P(), P())
    return jax.shard_map(shards, mesh=inner, in_specs=in_specs, out_specs=P(ORB, None), check_vma=False)
```

```python
import math

import jax
import jax.numpy as jnp
import ml_dtypes
import numpy as np
from jax import lax
from jax.experimental import pallas as pl
from jax.experimental.pallas import tpu as pltpu
from jax.sharding import Mesh, PartitionSpec as P

N = 80
PANEL = 64
GRID = ("zl", "yh", "yl", "c")
ORB = ("zh", "x")
ROWS = ("yh", "yl", "c")
PLANE = ("yl", "c", "x")
RING = ("yh", "zl", "zh")
BF16 = jnp.bfloat16
F32 = jnp.float32
LEVELS = 252.9
SPAN = 5.21
SHIFTS = (0, 1, 3, 2)
ROWS_A = 1280
ROWS_B = 720
FOUR_PI = 4.0 * math.pi
TWO_PI = 2.0 * math.pi


def real_basis():
    steps = np.arange(N)
    freqs = np.concatenate([np.arange(N // 2 + 1), np.arange(1, N // 2)])
    angle = TWO_PI / N * (freqs[:, None] * steps[None, :] % N)
    table = np.where(np.arange(N)[:, None] <= N // 2, np.cos(angle), np.sin(angle)) * math.sqrt(2.0 / N)
    table[0] /= math.sqrt(2.0)
    table[N // 2] /= math.sqrt(2.0)
    return table.astype(np.float32)


def freq_square(index):
    freq = jnp.where(index > N // 2, index - N // 2, index).astype(F32)
    wave = TWO_PI / N * freq
    return wave * wave


def mix(form, left, right):
    return jnp.einsum(form, left, right, precision=lax.Precision.HIGHEST, preferred_element_type=F32)


def swap(values, axes):
    return lax.all_to_all(values, axes, 0, 0, tiled=True)


def lane_power(square_sum, count):
    return jnp.ceil(0.5 * jnp.log2(jnp.maximum(square_sum * (1.0 / count), 1e-37))) - 1.0


def encode(values, power):
    size = jnp.abs(values) * jnp.exp2(-power)
    level = jnp.log(size + jnp.sqrt(size * size + 1.0)) * (LEVELS / SPAN)
    whole = jnp.floor(level)
    code = jnp.exp2(whole - 126.0) * (1.0 + (level - whole))
    return jnp.where(values < 0, -code, code)


def decode(code, power):
    size = jnp.abs(code)
    whole = jnp.floor(jnp.log2(size) + 1e-3)
    level = whole + (size * jnp.exp2(-whole) - 1.0) + 126.0
    spread = jnp.exp(level * (SPAN / LEVELS))
    value = 0.5 * (spread - 1.0 / spread) * jnp.exp2(power)
    return jnp.where(code < 0, -value, value)


def whole_call(kernel, out_shape, scratch, scalars, *arrays, flops=2 * 10**9):
    vmem = pl.BlockSpec(memory_space=pltpu.VMEM)
    shapes = [a.shape for a in arrays]
    moved = sum(math.prod(shape) * 4 for shape in shapes)
    return pl.pallas_call(
        kernel,
        out_shape=out_shape,
        in_specs=[pl.BlockSpec(memory_space=pltpu.SMEM)] * len(scalars) + [vmem] * len(arrays),
        out_specs=jax.tree.map(lambda _: vmem, out_shape),
        scratch_shapes=scratch,
        compiler_params=pltpu.CompilerParams(vmem_limit_bytes=40 * 2**20),
        cost_estimate=pl.CostEstimate(flops=flops, bytes_accessed=moved, transcendentals=0),
    )(*scalars, *arrays)


def head_rows(points_ref, shift, x_rank, panel):
    block = lax.rem(x_rank - shift + 4, 4)
    return jnp.concatenate([points_ref[(panel * 4 + i) * 4 + block] for i in range(4)], axis=0)


def side_table(head):
    half = head.shape[1] // 2
    gap = jnp.zeros((head.shape[0], half), head.dtype)
    upper = jnp.concatenate([head[:, :half], gap], axis=1)
    lower = jnp.concatenate([gap, head[:, half:]], axis=1)
    return jnp.concatenate([upper, lower], axis=0)


def dot_rows(left, right, precision=None):
    return lax.dot_general(left, right, (((1,), (1,)), ((), ())), precision=precision, preferred_element_type=F32)


def split(values):
    high = values.astype(BF16)
    return high, (values - high.astype(F32)).astype(BF16)


def dot_two(table_ref, values):
    high, low = split(values)
    count = table_ref.shape[0] // 2
    top, rest = table_ref[pl.ds(0, count), :], table_ref[pl.ds(count, count), :]
    return dot(top, high) + (dot(top, low) + dot(rest, high))


def dot(left, right):
    return lax.dot_general(left, right, (((1,), (0,)), ((), ())), preferred_element_type=F32)


def dot_three(left, right):
    (left, left_rest), (right, right_rest) = split(left), split(right)
    return dot(left, right) + (dot(left, right_rest) + dot(left_rest, right))


def two_parts(table):
    high = table.astype(ml_dtypes.bfloat16)
    low = (table - high.astype(np.float32)).astype(ml_dtypes.bfloat16)
    return jnp.asarray(np.concatenate([high, low], axis=0))


def sums_kernel(rank_ref, points_ref, own, left, right, far, one_ref, two_ref, sum_ref):
    panel_one = rank_ref[1]
    count = own.shape[0]
    tables = []
    for shift in SHIFTS:
        heads = [head_rows(points_ref, shift, rank_ref[0], panel) for panel in (panel_one, 1 - panel_one)]
        tables.append(jnp.concatenate([side_table(head) for head in heads], axis=0))
    tile = 320 if count == ROWS_A else 240
    tiles = [pl.ds(low, tile) for low in range(0, count, tile)]
    square = jnp.zeros((1, 4 * PANEL), F32)
    for rows in tiles:
        total = sum(dot_rows(block[rows, :], table) for block, table in zip((own, left, right, far), tables))
        sum_ref[rows, :] = total
        square = square + jnp.sum(total * total, axis=0, keepdims=True)
    power = lane_power(square, count)
    for out_ref, low in ((one_ref, 0), (two_ref, 2 * PANEL)):
        lanes = pl.ds(low, 2 * PANEL)
        own_power = power[:, low : low + 2 * PANEL]
        for rows in tiles:
            out_ref[rows, :] = encode(sum_ref[rows, lanes], own_power).astype(BF16)
        out_ref[pl.ds(count, 16), :] = jnp.broadcast_to(own_power, (16, 2 * PANEL)).astype(BF16)


def gram_kernel(rank_ref, points_ref, gram_ref):
    for panel in range(2):
        heads = [head_rows(points_ref, shift, rank_ref[0], panel) for shift in SHIFTS]
        gram_ref[pl.ds(panel * PANEL, PANEL), :] = sum(dot_rows(head, side_table(head)) for head in heads)


def first_kernel(below_a, above_a, below_b, above_b, basis_ref, out_ref):
    left_lanes = lax.broadcasted_iota(jnp.int32, (N, 2 * PANEL), 1) < PANEL
    out_ref[...] = jnp.zeros_like(out_ref)

    def product(column):
        refs, count = ((below_a, above_a), ROWS_A) if column < ROWS_A // N else ((below_b, above_b), ROWS_B)
        rows = pl.ds(column * N % ROWS_A, N)
        parts = [decode(ref[rows, :].astype(F32), ref[pl.ds(count, 16), :].astype(F32)[:1]) for ref in refs]
        sums = parts[0] + parts[1]
        return sums * pltpu.roll(sums, PANEL, 1)

    pairs = []
    for pair in range(13):
        right = product(pair + 13) if pair < 12 else 0.0
        pairs.append(jnp.where(left_lanes, product(pair), right))
    moved = dot_two(basis_ref, jnp.concatenate(pairs, axis=1))
    for pair in range(13):
        for k in range(5):
            rows = moved[k * 16 : k * 16 + 16, pair * 2 * PANEL : (pair + 1) * 2 * PANEL]
            out_ref[pl.ds(k * 16 + pair, 16, stride=80), :] = rows


def inverse_kernel(mine_ref, other_ref, fit_ref, bra_ref):
    sums = mine_ref[...] + other_ref[...]
    both = sums * pltpu.roll(sums, PANEL, 1)
    lane = lax.broadcasted_iota(jnp.int32, (PANEL, 2 * PANEL), 1)
    line = lax.broadcasted_iota(jnp.int32, (PANEL, 2 * PANEL), 0)
    left = lane < PANEL
    matrix = jnp.where(left, both[:PANEL], both[PANEL:])
    for step in range(PANEL):
        far = PANEL + step
        here = (lane == step) | (lane == far)
        row = matrix[step : step + 1]
        pivot = jnp.where(left[:1], row[:, step : step + 1], row[:, far : far + 1])
        row = jnp.where(here[:1], 1.0, row) / pivot
        column = jnp.where(left, matrix[:, step : step + 1], matrix[:, far : far + 1])
        rest = jnp.where(here, 0.0, matrix) - column * row
        matrix = jnp.where(line == step, row, rest)
    other = pltpu.roll(matrix, PANEL, 1)
    fit_ref[...] = jnp.where(left, matrix, other)
    bra_ref[...] = jnp.where(left, other, matrix)


def second_kernel(in_ref, table_ref, out_ref, line_ref, code_ref):
    left_lanes = lax.broadcasted_iota(jnp.int32, (200, 2 * PANEL), 1) < PANEL
    data = [in_ref[:, pl.ds(k * 16, 16), :].reshape(256, 2 * PANEL) for k in range(5)]
    moved = dot_two(table_ref, jnp.concatenate(data, axis=1))
    square = jnp.zeros((1, 2 * PANEL), F32)
    for k in range(5):
        part = moved[:, k * 2 * PANEL : (k + 1) * 2 * PANEL]
        low = part[:200] + pltpu.roll(part[200:400], PANEL, 1)
        high = pltpu.roll(part[400:600], PANEL, 1) + part[600:]
        mixed = jnp.where(left_lanes, low, high)
        line_ref[pl.ds(k * 200, 200), :] = mixed
        square = square + jnp.sum(mixed * mixed, axis=0, keepdims=True)
    power = lane_power(square, 1000)
    line_ref[pl.ds(1000, 120), :] = jnp.zeros((120, 2 * PANEL), F32)
    for tile in range(4):
        rows = pl.ds(tile * 280, 280)
        line_ref[rows, :] = encode(line_ref[rows, :], power)
    for to in range(32):
        code_ref[pl.ds(40 * to, 35), :] = line_ref[pl.ds(35 * to, 35), :]
        code_ref[pl.ds(40 * to + 35, 5), :] = jnp.broadcast_to(power, (5, 2 * PANEL))
    for tile in range(4):
        rows = pl.ds(tile * 320, 320)
        out_ref[rows, :] = code_ref[rows, :].astype(BF16)


def third_kernel(got_ref, table_ref, kernel_ref, fit_ref, bra_ref, out_ref):
    keep = lax.broadcasted_iota(jnp.int32, (40, 2 * PANEL), 0) < 35

    def side(panel):
        parts = []
        for source in range(16):
            block = got_ref[2 * source + (panel + (source % 8 < 4)) % 2].astype(F32)
            parts.append(jnp.where(keep, decode(jnp.where(keep, block, 1.0), block[35:36]), 0.0))
        return jnp.concatenate(parts, axis=0)

    moved = dot_two(table_ref, jnp.concatenate([side(0), side(1)], axis=1))
    fit_top, fit_rest = split(moved[:, : 2 * PANEL] * kernel_ref[...])
    bra_top, bra_rest = split(moved[:, 2 * PANEL :])

    def meet(left, right):
        return lax.dot_general(left, right, (((0,), (0,)), ((), ())), preferred_element_type=F32)

    total = meet(bra_top, fit_top) + (meet(bra_top, fit_rest) + meet(bra_rest, fit_top))
    total = total + pltpu.roll(pltpu.roll(total, PANEL, 0), PANEL, 1)
    total = dot_three(bra_ref[...][:, :PANEL], total[:PANEL, :PANEL])
    total = dot_three(total, fit_ref[...])
    left_lanes = lax.broadcasted_iota(jnp.int32, (4, 2 * PANEL), 1) < PANEL
    for to in range(4):
        for half in range(2):
            low = half * 32 + to * 8
            rows = jnp.where(left_lanes, total[low : low + 4], total[low + 4 : low + 8])
            for row in range(8):
                out_ref[row * 4 + to, pl.ds(half * 4, 4), :] = rows


def second_table():
    basis = real_basis().astype(np.float64)
    full = np.zeros((N, 5, 5 * N))
    for row in range(5):
        full[:, row, row * N : (row + 1) * N] = basis
    full = full.reshape(2, 200, 16, 25)
    table = np.zeros((2, 2, 200, 16, 16))
    table[:, 0, :, :, :13] = full[..., :13]
    table[:, 1, :, :, :12] = full[..., 13:]
    return table.reshape(800, 256).astype(np.float32)


def third_table():
    basis = np.roll(real_basis().reshape(N, 8, 2, 5).transpose(0, 2, 1, 3), 4, axis=2)
    table = np.zeros((7, N, 2, 8, 40), np.float32)
    for pair in range(7):
        table[pair, ..., pair * 5 : pair * 5 + 5] = basis
    return table.reshape(7 * N, 640)


def shards(occupied, virtual, points, panels):
    x_rank = lax.axis_index("x")
    zh_rank = lax.axis_index("zh")
    grid_rank = lax.axis_index(GRID)
    columns = occupied.shape[1]
    width = occupied.shape[2]
    per_x = columns // 4

    parts = jnp.concatenate([occupied, virtual], axis=2).reshape(N, 4, per_x, 2 * width)
    parts = parts.transpose(1, 2, 0, 3).reshape(4, per_x * N, 2 * width)

    wanted = panels.reshape(-1, 1) == jnp.arange(2 * PANEL, dtype=jnp.int32)
    chosen = jnp.sum(jnp.where(wanted, points, 0), axis=1)
    within = chosen % (N * N) - grid_rank * columns
    inside = (within >= 0) & (within < columns)
    plane_of = chosen // (N * N)
    column_of = jnp.where(inside, within, 0)
    here = jnp.concatenate([occupied[plane_of, column_of], virtual[plane_of, column_of]], axis=1)
    here = jnp.where(inside[:, None], here, jnp.zeros((), BF16))

    def take(shift):
        return lax.dynamic_index_in_dim(parts, (x_rank + shift) % 4, 0, keepdims=False)

    def spread(block, shift):
        return lax.ppermute(block, "x", [(i, (i + shift) % 4) for i in range(4)])

    whole = [take(shift) for shift in SHIFTS]
    first = [block[:ROWS_A] for block in whole]
    second = [block[ROWS_A:] for block in whole]
    first = first[:1] + [spread(block, shift) for block, shift in zip(first[1:], SHIFTS[1:])]

    def add(values):
        return jnp.sum(values.astype(F32), axis=0).astype(BF16)

    rows = add(swap(here.reshape(8, 16, 2 * width), ROWS))
    rows = add(swap(jnp.broadcast_to(rows[None], (8, 16, 2 * width)), "zl"))
    rows, first = lax.optimization_barrier((rows, first))
    pts = swap(jnp.broadcast_to(rows[None], (32, 16, 2 * width)), ROWS + ("x",))
    second = second[:1] + [spread(block, shift) for block, shift in zip(second[1:], SHIFTS[1:])]

    def cross(values):
        return lax.ppermute(values, "zh", [(0, 1), (1, 0)])

    def full(rows, dtype=F32, lanes=2 * PANEL):
        return jax.ShapeDtypeStruct((rows, lanes), dtype)

    ranks = jnp.stack([x_rank, (zh_rank + lax.axis_index("c")) % 2]).astype(jnp.int32)

    def hops(core_zero):
        pairs = []
        for z in range(16):
            for core, step in ((0, core_zero), (1, 16 - core_zero)):
                to = (z + step) % 16
                pairs.append((((z % 8) * 2 + core) * 2 + z // 8, ((to % 8) * 2 + core) * 2 + to // 8))
        return pairs

    def half_sums(points, blocks):
        count = blocks[0].shape[0]
        outs = (full(count + 16, BF16), full(count + 16, BF16))
        scratch = [pltpu.VMEM((count, 4 * PANEL), F32)]
        one, two = whole_call(sums_kernel, outs, scratch, (ranks,), points, *blocks)
        return one, lax.ppermute(one, ("zl", "c", "zh"), hops(4)), lax.ppermute(two, ("zl", "c", "zh"), hops(12))

    one, *got_a = half_sums(pts, first)
    _, *got_b = half_sums(pts, second)
    pts, one = lax.optimization_barrier((pts, one))
    gram = whole_call(gram_kernel, full(2 * PANEL), [], (ranks,), pts, flops=0)
    other_gram = cross(gram)

    basis_a = real_basis().reshape(16, 5, N).transpose(1, 0, 2).reshape(N, N)
    fields = whole_call(first_kernel, full(16 * 80), [], (), *got_a, *got_b, two_parts(basis_a))
    fields = swap(fields.reshape(16, 80, 2 * PANEL), PLANE)
    scratch = [pltpu.VMEM((1120, 2 * PANEL), F32), pltpu.VMEM((1280, 2 * PANEL), F32)]
    fields = whole_call(second_kernel, full(1280, BF16), scratch, (), fields, two_parts(second_table()))
    fields, gram, other_gram = lax.optimization_barrier((fields, gram, other_gram))
    inverses = whole_call(inverse_kernel, (full(PANEL), full(PANEL)), [], (), gram, other_gram)
    fields = swap(fields.reshape(32, 40, 2 * PANEL), RING)

    slot = lax.axis_index(RING) * 7 + jnp.arange(7, dtype=jnp.int32)
    square_a = freq_square(lax.axis_index(PLANE) * 5 + slot // 40)
    square_c = freq_square(slot[:, None] % 40 + jnp.arange(2, dtype=jnp.int32)[None, :] * 40)
    square_b = freq_square(jnp.arange(N, dtype=jnp.int32))
    squared = square_a[:, None, None] + square_b[None, :, None] + square_c[:, None, :]
    live = (squared > 0) & (slot < 200)[:, None, None]
    kernel = jnp.where(live, 32.0 * FOUR_PI / jnp.where(squared > 0, squared, 1.0), 0.0)
    kernel = jnp.broadcast_to(kernel[..., None], (7, N, 2, PANEL)).reshape(7 * N, 2 * PANEL)
    out_shape = jax.ShapeDtypeStruct((32, 8, 2 * PANEL), F32)
    part = whole_call(third_kernel, out_shape, [], (), fields, two_parts(third_table()), kernel, *inverses)
    part = jnp.sum(swap(part, ROWS + ("x",)), axis=0)
    part = jnp.broadcast_to(part.reshape(1, 2, 4, 2 * PANEL), (8, 2, 4, 2 * PANEL)).reshape(16, 4, 2 * PANEL)
    part = jnp.sum(swap(part, ("zl", "zh")), axis=0)
    return jnp.concatenate([part[:, :PANEL], part[:, PANEL:]], axis=0)


def solution(mesh):
    devices = mesh.devices.reshape(8, 2, 2, 2, 2, 4)
    inner = Mesh(devices, ("zl", "yh", "yl", "c", "zh", "x"))
    in_specs = (P(None, GRID, ORB), P(None, GRID, ORB), P(), P())
    return jax.shard_map(shards, mesh=inner, in_specs=in_specs, out_specs=P(ORB, None), check_vma=False)
```
